512 devices in a mesh: pipe: 32 (over y, x_lo, core), ctx: 16 (over z, x_hi).
Axes of the slice: x: 4 (x_hi: 2, x_lo: 2; x = x_hi * 2 + x_lo), y: 8, z: 8, core: 2. Of those that a mesh axis runs over, the one named last changes fastest.
Arguments:
- queries: bfloat16 [32, 128, 36864], P('pipe', 'ctx')
- out_grad: bfloat16 [32, 128, 32768], P('pipe', 'ctx'), may hold values from -6 to 6
- latent: bfloat16 [32, 2048, 512], P('pipe', 'ctx')
- rope_keys: bfloat16 [32, 2048, 64], P('pipe', 'ctx'), may hold values from -6 to 6
- gain: float32 [16, 512], replicated, may hold values from 0.5 to 2
- block_map: int32 [32, 32], P('pipe', 'ctx'), may hold values from 0 to 31, as said below
- query_start: int32 [32, 16], P('pipe', 'ctx'), may hold values from 64 to 2040, as said below
Outputs:
- attended: bfloat16 [32, 128, 32768], P('pipe', 'ctx')
- query_grad: bfloat16 [32, 128, 36864], P('pipe', 'ctx')
- latent_grad: bfloat16 [32, 2048, 512], P('pipe', 'ctx')
- rope_grad: bfloat16 [32, 2048, 64], P('pipe', 'ctx')
- gain_grad: float32 [32, 512], P('pipe')
The draws below stay inside these ranges and needn't reach their ends.
Inputs may be any that keep to these rules, and one draw needn't show every extreme that they name: `block_map`: each row is an ordering of the 32 blocks: every block once. Slot t lies on ctx device t // 2. `query_start`: A device's 8 queries lie inside the later, in sequence order, of the two blocks in its slots; the device holding the last block has its queries at that block's end.
All inputs are finite; a program needn't handle non-finite values.
Results may differ from the reference program's by a relative error of at most 0.02.
Values may be sent and summed in bfloat16 or wider, within the bound.
No kernel may reach another device: no remote copies, remote signals or barrier semaphores. Data moves between devices by JAX's collectives and lax.ppermute only.
A program may use at most 64 MiB of HBM per device.

```python
import math
import jax
import jax.numpy as jnp
from jax import lax

HEADS = 64
DL = 512
DR = 64
QKW = 576
TQ_DEV = 8
TK_DEV = 128
MICRO = 32
SECTIONS = 16
KEYS = 2048
QROWS = 128
NBLK = 32
N_CTX = 16


def shared_base(key):
    return jax.random.normal(key, (MICRO, KEYS, DL), jnp.float32)


def shared_blocks(key):
    block_key = jax.random.fold_in(key, 101)
    micro_keys = jax.random.split(block_key, MICRO)
    return jax.vmap(lambda one_key: jax.random.permutation(one_key, NBLK))(micro_keys).astype(jnp.int32)


def draw_block_map(key, part):
    return shared_blocks(key)


def draw_query_start(key, part):
    orders = shared_blocks(key)
    key = jax.random.fold_in(key, 2)
    block_len = TK_DEV // 2
    paired = orders.reshape(MICRO, NBLK // 2, 2)
    later = jnp.max(paired, axis=2)
    span_len = block_len - TQ_DEV + 1
    offsets = jax.random.randint(key, (MICRO, NBLK // 2), 0, span_len).astype(jnp.int32)
    offsets = jnp.where(later == NBLK - 1, span_len - 1, offsets)
    return (later * block_len + offsets).astype(jnp.int32)


def draw_latent(key, part):
    base_rows = shared_base(key)
    return base_rows.astype(jnp.bfloat16)


def draw_queries(key, part):
    key = jax.random.fold_in(key, 4)
    noise = jax.random.normal(key, (MICRO, QROWS, HEADS, QKW), jnp.float32)
    return noise.reshape(MICRO, QROWS, HEADS * QKW).astype(jnp.bfloat16)


def level_of(stream_key, extent, shards, least, high):
    level = 1.0
    for dim, blocks in shards:
        draws = jax.random.uniform(jax.random.fold_in(jax.random.fold_in(stream_key, 6), dim), (blocks,), jnp.float32, least / len(shards), high / len(shards))
        level = level * jnp.repeat(jnp.exp(draws), extent[dim] // blocks).reshape((-1,) + (1,) * (len(extent) - 1 - dim))
    return level


def centred(rng, extent, width, most, cuts=(), kind=jnp.bfloat16):
    values = jax.random.normal(rng, extent, jnp.float32) * width
    if len(cuts) > 0:
        values = level_of(rng, extent, cuts, -0.22, 0.18) * values
    return jnp.clip(values, min=-most, max=most).astype(kind)


def setup_inputs(seed: int = 0) -> dict:
    keys = jax.random.split(jax.random.key(seed), 8)
    return {
        "queries": draw_queries(jax.random.fold_in(keys[7], 71), 0),
        "out_grad": centred(keys[1], (MICRO, QROWS, HEADS * DL), 1.0, 6.0, ((0, 32), (1, 16))),
        "latent": draw_latent(jax.random.fold_in(keys[7], 71), 0),
        "rope_keys": centred(keys[3], (MICRO, KEYS, DR), 1.0, 6.0, ((0, 32), (1, 16))),
        "gain": jnp.clip(jnp.exp(jax.random.uniform(keys[4], (SECTIONS, DL), jnp.float32, math.log(0.5), math.log(2.0))), 0.5, 2.0),
        "block_map": draw_block_map(jax.random.fold_in(keys[7], 71), 0),
        "query_start": draw_query_start(jax.random.fold_in(keys[7], 71), 0),
    }


score_scale = 1.0 / math.sqrt(192.0)

def one_micro(queries, out_grad, latent, rope_keys, gain_row, block_map, query_start):
    block_len = KEYS // NBLK
    latent_f = latent.astype(jnp.float32)
    inverse = lax.rsqrt(lax.optimization_barrier(jnp.mean(latent_f * latent_f, axis=-1, keepdims=True)) + 1e-06)
    normal_unit = latent_f * inverse
    key_rows = jnp.concatenate([normal_unit * gain_row[None, :], rope_keys.astype(jnp.float32)], axis=1).astype(jnp.bfloat16)
    key_pos = (block_map[:, None] * block_len + jnp.arange(block_len, dtype=jnp.int32)[None, :]).reshape(-1)
    query_rows = queries.reshape(QROWS * HEADS, QKW)
    query_pos = (query_start[:, None] + jnp.arange(TQ_DEV, dtype=jnp.int32)[None, :]).reshape(-1)
    row_pos = jnp.repeat(query_pos, HEADS)
    scores = jnp.dot(query_rows, key_rows.T, preferred_element_type=jnp.float32) * score_scale
    visible = key_pos[None, :] <= row_pos[:, None]
    scores = jnp.where(visible, scores, -jnp.inf)
    row_max = lax.optimization_barrier(jnp.max(scores, axis=1, keepdims=True))
    expsum = jnp.exp(scores - row_max)
    weights_f = expsum / lax.optimization_barrier(jnp.sum(expsum, axis=1, keepdims=True))
    weights_b = weights_f.astype(jnp.bfloat16)
    value_rows = key_rows[:, :DL]
    attended = jnp.dot(weights_b, value_rows, preferred_element_type=jnp.float32).astype(jnp.bfloat16)
    grad_rows = out_grad.reshape(QROWS * HEADS, DL)
    dprob = jnp.dot(grad_rows, value_rows.T, preferred_element_type=jnp.float32)
    row_delta = lax.optimization_barrier(jnp.sum(grad_rows.astype(jnp.float32) * attended.astype(jnp.float32), axis=1, keepdims=True))
    dscore = (weights_f * (dprob - row_delta) * score_scale).astype(jnp.bfloat16)
    query_grad = jnp.dot(dscore, key_rows, preferred_element_type=jnp.float32).astype(jnp.bfloat16)
    per_dev = TQ_DEV * HEADS
    dscore_c = dscore.reshape(N_CTX, per_dev, KEYS).astype(jnp.float32)
    query_c = query_rows.reshape(N_CTX, per_dev, QKW).astype(jnp.float32)
    weights_c = weights_b.reshape(N_CTX, per_dev, KEYS).astype(jnp.float32)
    grads_c = grad_rows.reshape(N_CTX, per_dev, DL).astype(jnp.float32)
    score_term = jnp.einsum('cqk,cqd->ckd', dscore_c, query_c)
    value_term = jnp.einsum('cqk,cqd->ckd', weights_c, grads_c)
    value_term = jnp.pad(value_term, ((0, 0), (0, 0), (0, DR)))
    key_term = (score_term + value_term).astype(jnp.bfloat16).astype(jnp.float32)
    key_grad = lax.optimization_barrier(jnp.sum(key_term, axis=0))
    g_part = key_grad[:, :DL]
    rope_grad = key_grad[:, DL:].astype(jnp.bfloat16)
    gated = g_part * gain_row[None, :]
    latent_grad = (inverse * gated - latent_f * inverse ** 3 * lax.optimization_barrier(jnp.mean(gated * latent_f, axis=-1, keepdims=True))).astype(jnp.bfloat16)
    gain_part = lax.optimization_barrier(jnp.sum(g_part * normal_unit, axis=0))
    return (attended.reshape(QROWS, HEADS * DL), query_grad.reshape(QROWS, HEADS * QKW), latent_grad, rope_grad, gain_part)

def reference(queries, out_grad, latent, rope_keys, gain, block_map, query_start):

    def step_micro(micro_index):
        section_row = jnp.minimum(micro_index, MICRO - 1 - micro_index)
        gain_row = lax.dynamic_index_in_dim(gain, section_row, 0, keepdims=False)
        return one_micro(queries[micro_index], out_grad[micro_index], latent[micro_index], rope_keys[micro_index], gain_row, block_map[micro_index], query_start[micro_index])
    attended, query_grad, latent_grad, rope_grad, gain_part = lax.map(step_micro, jnp.arange(MICRO, dtype=jnp.int32))
    gain_grad = gain_part + gain_part[::-1]
    return (attended, query_grad, latent_grad, rope_grad, gain_grad)
```

```python
import math

import jax
import jax.numpy as jnp
from jax import lax
from jax.experimental import pallas as pl
from jax.experimental.pallas import tpu as pltpu
from jax.sharding import Mesh, PartitionSpec as P

HEADS = 64
DL = 512
DR = 64
QKW = DL + DR
WIDE = 640
BLOCK = 64
CHUNK = 256
SCORE_SCALE = 1.0 / math.sqrt(192.0)
F32 = jnp.float32
BF16 = jnp.bfloat16
VMEM = pl.BlockSpec(memory_space=pltpu.VMEM)
SMEM = pl.BlockSpec(memory_space=pltpu.SMEM)


def params():
    return pltpu.CompilerParams(vmem_limit_bytes=48 * 1024 * 1024)


def section_gain(gain_ref, section_ref):
    return gain_ref[pl.ds(section_ref[0], 1), :]


def key_kernel(section_ref, latent_ref, rope_ref, gain_ref, keys_ref):
    latent = latent_ref[...].astype(F32)
    inverse = lax.rsqrt(jnp.mean(latent * latent, axis=-1, keepdims=True) + 1e-06)
    keys_ref[:, :DL] = (latent * inverse * section_gain(gain_ref, section_ref)).astype(BF16)
    keys_ref[:, DL:QKW] = rope_ref[...]
    keys_ref[:, QKW:] = jnp.zeros((keys_ref.shape[0], WIDE - QKW), BF16)


def nt_dot(a, b):
    return lax.dot_general(a, b, (((1,), (1,)), ((), ())), preferred_element_type=F32)


def tn_dot(a, b):
    return lax.dot_general(a, b, (((0,), (0,)), ((), ())), preferred_element_type=F32)


def fold(value, combine):
    parts = [value[i * 8 : (i + 1) * 8] for i in range(value.shape[0] // 8)]
    while len(parts) > 1:
        half = len(parts) // 2
        parts = [combine(parts[i], parts[half + i]) for i in range(half)]
    return parts[0]


def core_kernel(
    blocks_ref, place_ref, q_ref, do_ref, k_ref, kg_ref, w_ref, ds_ref, s_ref, dp_ref
):
    keys, rows = s_ref.shape
    query_start, my_x = place_ref[0], place_ref[1]
    chunks = keys // CHUNK
    groups = CHUNK // BLOCK
    token = lax.broadcasted_iota(jnp.int32, (BLOCK, rows), 1) // HEADS
    lead = lax.broadcasted_iota(jnp.int32, (BLOCK, rows), 0) - token
    top = None
    for c in range(chunks):
        at = pl.ds(c * CHUNK, CHUNK)
        scores = nt_dot(k_ref[at, :], q_ref[...])
        pieces = []
        for g in range(groups):
            room = query_start - blocks_ref[c * groups + g] * BLOCK
            piece = scores[g * BLOCK : (g + 1) * BLOCK] * SCORE_SCALE
            pieces.append(jnp.where(lead <= room, piece, -jnp.inf))
        scores = jnp.concatenate(pieces, axis=0)
        s_ref[at, :] = scores
        part = fold(scores, jnp.maximum)
        top = part if top is None else jnp.maximum(top, part)
    top = jnp.max(top, axis=0, keepdims=True)
    total = jnp.zeros((8, rows), F32)
    pull = jnp.zeros((8, rows), F32)
    for c in range(chunks):
        at = pl.ds(c * CHUNK, CHUNK)
        dprob = nt_dot(k_ref[at, :DL], do_ref[...])
        expo = jnp.exp(s_ref[at, :] - top)
        s_ref[at, :] = expo
        dp_ref[at, :] = dprob
        total = total + fold(expo, jnp.add)
        pull = pull + fold(expo * dprob, jnp.add)
    scale = 1.0 / jnp.sum(total, axis=0, keepdims=True)
    delta = jnp.sum(pull, axis=0, keepdims=True) * scale
    for c in range(chunks):
        at = pl.ds(c * CHUNK, CHUNK)
        weights = s_ref[at, :] * scale
        dscore = (weights * (dp_ref[at, :] - delta) * SCORE_SCALE).astype(BF16)
        weights = weights.astype(BF16)
        w_ref[at, :] = weights
        ds_ref[at, :] = dscore
        lat = jnp.dot(dscore, q_ref[:, :DL], preferred_element_type=F32)
        lat = lat + jnp.dot(weights, do_ref[...], preferred_element_type=F32)
        rope = jnp.dot(dscore, q_ref[:, DL:], preferred_element_type=F32)
        for half in range(2):
            to = pl.ds(pl.multiple_of(c * CHUNK + 128 * (half ^ my_x), 128), 128)
            kg_ref[to, :DL] = lat[half * 128 : half * 128 + 128].astype(BF16)
            kg_ref[to, DL:] = rope[half * 128 : half * 128 + 128].astype(BF16)


def query_kernel(
    section_ref, w_ref, ds_ref, k_ref, q_ref, do_ref, gain_ref, att_ref, dq_ref, part_ref
):
    att = tn_dot(w_ref[...], k_ref[:, :DL])
    dq = tn_dot(ds_ref[...], k_ref[...])
    att_ref[...] = att.astype(BF16)
    dq_ref[...] = dq[:, :QKW].astype(BF16)
    terms = q_ref[:, :DL].astype(F32) * dq[:, :DL] + do_ref[...].astype(F32) * att
    part = jnp.sum(fold(terms, jnp.add), axis=0, keepdims=True)
    part_ref[...] = part / section_gain(gain_ref, section_ref)


def grad_kernel(section_ref, own_ref, far_ref, latent_ref, gain_ref, lg_ref, rg_ref):
    gain = section_gain(gain_ref, section_ref)
    latent = latent_ref[...].astype(F32)
    inverse = lax.rsqrt(jnp.mean(latent * latent, axis=-1, keepdims=True) + 1e-06)
    total = own_ref[...].astype(F32) + far_ref[...].astype(F32)
    gated = total[:, :DL] * gain
    mean = jnp.mean(gated * latent, axis=-1, keepdims=True)
    lg_ref[...] = (inverse * gated - latent * (inverse * inverse * inverse) * mean).astype(BF16)
    rg_ref[...] = total[:, DL:QKW].astype(BF16)


def shards(queries, out_grad, latent, rope_keys, gain, block_map, query_start):
    tokens = queries.shape[1]
    rows = tokens * HEADS
    own = latent.shape[1]
    n_pipe = lax.axis_size("pipe")
    n_z = lax.axis_size("z")
    n_x = lax.axis_size("x")
    keys = own * n_z * n_x
    pipe = lax.axis_index("pipe")
    section = jnp.minimum(pipe, n_pipe - 1 - pipe).reshape(1)
    place = jnp.stack([query_start[0, 0], lax.axis_index("x")])

    local = pl.pallas_call(
        key_kernel,
        out_shape=jax.ShapeDtypeStruct((own, WIDE), BF16),
        in_specs=[SMEM, VMEM, VMEM, VMEM],
        out_specs=VMEM,
        compiler_params=params(),
    )(section, latent[0], rope_keys[0], gain)
    pair = lax.all_gather(local, "x", axis=0, tiled=True)
    key_rows = lax.all_gather(pair, "z", axis=0, tiled=True)
    blocks = lax.all_gather(block_map[0], ("z", "x"), axis=0, tiled=True)

    q = jnp.pad(queries[0].reshape(rows, QKW), ((0, 0), (0, WIDE - QKW)))
    do = out_grad[0].reshape(rows, DL)
    kg, w, ds = pl.pallas_call(
        core_kernel,
        out_shape=(
            jax.ShapeDtypeStruct((keys, WIDE), BF16),
            jax.ShapeDtypeStruct((keys, rows), BF16),
            jax.ShapeDtypeStruct((keys, rows), BF16),
        ),
        in_specs=[SMEM, SMEM, VMEM, VMEM, VMEM],
        out_specs=(VMEM, VMEM, VMEM),
        scratch_shapes=[pltpu.VMEM((keys, rows), F32), pltpu.VMEM((keys, rows), F32)],
        compiler_params=params(),
        cost_estimate=pl.CostEstimate(
            flops=2 * keys * rows * (2 * WIDE + 2 * DL), bytes_accessed=10**7, transcendentals=keys * rows
        ),
    )(blocks, place, q, do, key_rows)
    mine = lax.psum_scatter(kg, "z", scatter_dimension=0, tiled=True)

    att, dq, part = pl.pallas_call(
        query_kernel,
        out_shape=(
            jax.ShapeDtypeStruct((rows, DL), BF16),
            jax.ShapeDtypeStruct((rows, QKW), BF16),
            jax.ShapeDtypeStruct((1, DL), F32),
        ),
        in_specs=[SMEM] + [VMEM] * 6,
        out_specs=(VMEM, VMEM, VMEM),
        compiler_params=params(),
        cost_estimate=pl.CostEstimate(
            flops=2 * keys * rows * (WIDE + DL), bytes_accessed=10**7, transcendentals=0
        ),
    )(section, w, ds, key_rows, q, do, gain)

    def swap(value, axis, mask):
        size = lax.axis_size(axis)
        return lax.ppermute(value, axis, [(i, i ^ mask) for i in range(size)])

    part = part + swap(part, "pipe", n_pipe - 1)
    part = part + swap(part, "x", 1)
    for bit in (1, 2, 4):
        part = part + swap(part, "z", bit)

    far = swap(mine[own:], "x", 1)
    latent_grad, rope_grad = pl.pallas_call(
        grad_kernel,
        out_shape=(
            jax.ShapeDtypeStruct((own, DL), BF16),
            jax.ShapeDtypeStruct((own, DR), BF16),
        ),
        in_specs=[SMEM] + [VMEM] * 4,
        out_specs=(VMEM, VMEM),
        compiler_params=params(),
    )(section, mine[:own], far, latent[0], gain)
    return (
        att.reshape(1, tokens, HEADS * DL),
        dq.reshape(1, tokens, HEADS * QKW),
        latent_grad[None],
        rope_grad[None],
        part,
    )


def solution(mesh):
    n_pipe, n_ctx = mesh.devices.shape
    split = Mesh(mesh.devices.reshape(n_pipe, n_ctx // 2, 2), ("pipe", "z", "x"))
    tokens = P("pipe", ("z", "x"), None)
    ints = P("pipe", ("z", "x"))
    return jax.shard_map(
        shards,
        mesh=split,
        in_specs=(tokens, tokens, tokens, tokens, P(), ints, ints),
        out_specs=(tokens, tokens, tokens, tokens, P("pipe", None)),
        check_vma=False,
    )
```

```python
import math

import jax
import jax.numpy as jnp
from jax import lax
from jax.experimental import pallas as pl
from jax.experimental.pallas import tpu as pltpu
from jax.sharding import Mesh, PartitionSpec as P

HEADS = 64
DL = 512
DR = 64
QKW = DL + DR
WIDE = 640
BLOCK = 64
SCORE_SCALE = 1.0 / math.sqrt(192.0)
F32 = jnp.float32
BF16 = jnp.bfloat16
VMEM = pl.BlockSpec(memory_space=pltpu.VMEM)
SMEM = pl.BlockSpec(memory_space=pltpu.SMEM)


def call(kernel, out, ins, args):
    return pl.pallas_call(
        kernel,
        out_shape=out,
        in_specs=ins,
        out_specs=jax.tree.map(lambda _: VMEM, out),
        compiler_params=pltpu.CompilerParams(vmem_limit_bytes=16 * 1024 * 1024),
        cost_estimate=pl.CostEstimate(flops=1, bytes_accessed=1, transcendentals=0),
    )(*args)


def shape(rows, columns, dtype):
    return jax.ShapeDtypeStruct((rows, columns), dtype)


def nt_dot(a, b):
    return lax.dot_general(a, b, (((1,), (1,)), ((), ())), preferred_element_type=F32)


def tn_dot(a, b):
    return lax.dot_general(a, b, (((0,), (0,)), ((), ())), preferred_element_type=F32)


def mm(a, b):
    return jnp.dot(a, b, preferred_element_type=F32)


def section_gain(gain_ref, section_ref):
    return gain_ref[pl.ds(section_ref[0], 1), :]


def fold(value, combine):
    parts = [value[i * 8 : (i + 1) * 8] for i in range(value.shape[0] // 8)]
    while len(parts) > 1:
        half = len(parts) // 2
        parts = [combine(parts[i], parts[half + i]) for i in range(half)]
    return parts[0]


def key_kernel(section_ref, blocks_ref, latent_ref, rope_ref, gain_ref, keys_ref):
    own = keys_ref.shape[0]
    latent = latent_ref[...].astype(F32)
    inverse = lax.rsqrt(jnp.mean(latent * latent, axis=-1, keepdims=True) + 1e-06)
    keys_ref[:, :DL] = (latent * inverse * section_gain(gain_ref, section_ref)).astype(BF16)
    keys_ref[:, DL:QKW] = rope_ref[...]
    first = lax.broadcasted_iota(jnp.int32, (own, WIDE - QKW), 0) < BLOCK
    blocks = jnp.where(first, blocks_ref[0, 0], blocks_ref[0, 1])
    keys_ref[:, QKW:] = blocks.astype(F32).astype(BF16)


def masked_scores(q_pos, q_ref, k_ref):
    count = k_ref.shape[0]
    scores = nt_dot(k_ref[...], q_ref[...]) * SCORE_SCALE
    place = (lax.broadcasted_iota(jnp.int32, (count, 1), 0) % BLOCK).astype(F32)
    k_pos = k_ref[:, QKW : QKW + 1].astype(F32) * BLOCK + place
    return jnp.where(k_pos <= q_pos, scores, -jnp.inf)


def stats_kernel(first, parts, *refs):
    pos_ref, q_ref, do_ref = refs[:3]
    k_refs = refs[3 : 3 + parts]
    out_ref = refs[-1]
    q_pos = pos_ref[0:1, :]
    scores = [masked_scores(q_pos, q_ref, k_ref) for k_ref in k_refs]
    top = fold(jnp.concatenate([fold(s, jnp.maximum) for s in scores]), jnp.maximum)
    top = jnp.max(top, axis=0, keepdims=True)
    if not first:
        old = refs[3 + parts]
        top = jnp.maximum(top, old[0:1, :])
    total, pull = 0.0, 0.0
    for s, k_ref in zip(scores, k_refs):
        dprob = nt_dot(k_ref[:, :DL], do_ref[...])
        expo = jnp.exp(s - top)
        total = total + fold(expo, jnp.add)
        pull = pull + fold(expo * dprob, jnp.add)
    total = jnp.sum(total, axis=0, keepdims=True)
    pull = jnp.sum(pull, axis=0, keepdims=True)
    if not first:
        shrink = jnp.exp(old[0:1, :] - top)
        total = total + old[1:2, :] * shrink
        pull = pull + old[2:3, :] * shrink
    out_ref[0:1, :] = top
    out_ref[1:2, :] = total
    out_ref[2:3, :] = pull


def weigh(stats_ref, q_pos, q_ref, do_ref, k_ref):
    scale = 1.0 / stats_ref[1:2, :]
    delta = stats_ref[2:3, :] * scale
    scores = masked_scores(q_pos, q_ref, k_ref)
    dprob = nt_dot(k_ref[:, :DL], do_ref[...])
    weights = jnp.exp(scores - stats_ref[0:1, :]) * scale
    dscore = (weights * (dprob - delta) * SCORE_SCALE).astype(BF16)
    return weights.astype(BF16), dscore


def key_grad_kernel(parts, *refs):
    pos_ref, stats_ref, q_ref, do_ref = refs[:4]
    k_refs = refs[4 : 4 + parts]
    kg_refs = refs[4 + parts : 4 + 2 * parts]
    gain_sum = 0.0
    for k_ref, kg_ref in zip(k_refs, kg_refs):
        weights, dscore = weigh(stats_ref, pos_ref[0:1, :], q_ref, do_ref, k_ref)
        lat = mm(dscore, q_ref[:, :DL]) + mm(weights, do_ref[...])
        kg_ref[:, :DL] = lat.astype(BF16)
        kg_ref[:, DL:] = mm(dscore, q_ref[:, DL:]).astype(BF16)
        gain_sum = gain_sum + fold(lat * k_ref[:, :DL].astype(F32), jnp.add)
    refs[-1][...] = gain_sum


def query_side_kernel(parts, first, *refs):
    pos_ref, stats_ref, q_ref, do_ref = refs[:4]
    k_refs = refs[4 : 4 + parts]
    att_ref, dq_ref = refs[-2:]
    att, dq = (0.0, 0.0) if first else (refs[4 + parts][...], refs[5 + parts][...])
    for k_ref in k_refs:
        weights, dscore = weigh(stats_ref, pos_ref[0:1, :], q_ref, do_ref, k_ref)
        att = att + tn_dot(weights, k_ref[:, :DL])
        dq = dq + tn_dot(dscore, k_ref[...])
    att_ref[...] = att.astype(att_ref.dtype)
    dq_ref[...] = dq[:, : dq_ref.shape[1]].astype(dq_ref.dtype)


def spread(vector):
    high = vector.astype(BF16).astype(F32)
    rows = [part[:, i : i + 64] for part in (high, vector - high) for i in range(0, DL, 64)]
    return jnp.concatenate(rows, axis=0).astype(BF16)


def gathered(ref):
    both = ref[0:16, QKW:].astype(F32)
    both = both[0:8] + both[8:16]
    return jnp.concatenate([both[i : i + 1] for i in range(8)], axis=1)


def gain_kernel(section_ref, gain_ref, *refs):
    total = refs[0][...]
    for ref in refs[1:-2]:
        total = total + ref[...]
    vector = jnp.sum(total, axis=0, keepdims=True) / section_gain(gain_ref, section_ref)
    refs[-2][...] = vector
    refs[-1][...] = spread(vector)


def add_kernel(half, here_ref, come_ref, *refs):
    out_ref = refs[-1]
    if half is None:
        out_ref[...] = (here_ref[...].astype(F32) + come_ref[...].astype(F32)).astype(BF16)
    else:
        own = come_ref.shape[0]
        at, rest = pl.ds(half * own, own), pl.ds((1 - half) * own, own)
        out_ref[at, :] = (here_ref[at, :].astype(F32) + come_ref[...].astype(F32)).astype(BF16)
        out_ref[rest, :] = here_ref[rest, :]
    if len(refs) > 1:
        out_ref[0:16, QKW:] = refs[0][...]


def near_kernel(own_ref, right_ref, left_ref, out_ref):
    out_ref[...] = own_ref[...] + gathered(right_ref) + gathered(left_ref)


def total_kernel(
    x_ref, right_ref, left_ref, here_ref, near_ref, across_ref, own_ref, far_ref, sum_ref
):
    own = own_ref.shape[0]
    for ref, place in ((own_ref, x_ref[0]), (far_ref, 1 - x_ref[0])):
        at = pl.ds(pl.multiple_of(place * own, own), own)
        ref[...] = (
            right_ref[at, :].astype(F32) + left_ref[at, :].astype(F32) + here_ref[at, :].astype(F32)
        ).astype(ref.dtype)
    total = near_ref[...] + across_ref[...] + gathered(right_ref) + gathered(left_ref)
    sum_ref[...] = total
    far_ref[0:16, QKW:] = spread(total)


def latent_kernel(section_ref, own_ref, far_ref, latent_ref, gain_ref, sum_ref, lg_ref, rg_ref, gg_ref):
    gain = section_gain(gain_ref, section_ref)
    latent = latent_ref[...].astype(F32)
    inverse = lax.rsqrt(jnp.mean(latent * latent, axis=-1, keepdims=True) + 1e-06)
    total = own_ref[...] + far_ref[...].astype(F32)
    gated = total[:, :DL] * gain
    mean = jnp.mean(gated * latent, axis=-1, keepdims=True)
    lg_ref[...] = (inverse * gated - latent * (inverse * inverse * inverse) * mean).astype(BF16)
    rg_ref[...] = total[:, DL:QKW].astype(BF16)
    gg_ref[...] = sum_ref[...] + gathered(far_ref)


def after(value, *first):
    return lax.optimization_barrier((value, *first))


def swap(value, axis, mask):
    size = lax.axis_size(axis)
    return lax.ppermute(value, axis, [(i, i ^ mask) for i in range(size)])


def shards(queries, out_grad, latent, rope_keys, gain, block_map, query_start):
    tokens = queries.shape[1]
    rows = tokens * HEADS
    own = latent.shape[1]
    n_pipe = lax.axis_size("pipe")
    n_z = lax.axis_size("z")
    pipe = lax.axis_index("pipe")
    section = jnp.minimum(pipe, n_pipe - 1 - pipe).reshape(1)
    place = lax.axis_index("x").reshape(1)

    def right(value):
        return lax.ppermute(value, "z", [(i, (i + 1) % n_z) for i in range(n_z)])

    def left(value):
        return lax.ppermute(value, "z", [(i, (i - 1) % n_z) for i in range(n_z)])

    local = call(
        key_kernel,
        shape(own, WIDE, BF16),
        [SMEM, SMEM, VMEM, VMEM, VMEM],
        (section, block_map, latent[0], rope_keys[0], gain),
    )
    pair = lax.all_gather(local, "x", axis=0, tiled=True)
    q = jnp.pad(queries[0].reshape(rows, QKW), ((0, 0), (0, WIDE - QKW)))
    do = out_grad[0].reshape(rows, DL)
    token = jnp.arange(8 * rows, dtype=jnp.int32).reshape(8, rows) % rows // HEADS
    q_pos = (query_start[0, 0] + token).astype(F32)

    def take_stats(held, stats):
        args = [q_pos, q, do, *held] + ([] if stats is None else [stats])
        return call(
            lambda *refs: stats_kernel(stats is None, len(held), *refs),
            shape(8, rows, F32),
            [VMEM] * len(args),
            args,
        )

    def key_grads(held):
        args = [q_pos, stats, q, do, *held]
        return call(
            lambda *refs: key_grad_kernel(len(held), *refs),
            [shape(piece.shape[0], WIDE, BF16) for piece in held] + [shape(8, DL, F32)],
            [VMEM] * len(args),
            args,
        )

    def query_side(held, sums, last=False):
        args = [q_pos, stats, q, do, *held, *sums]
        dtype = BF16 if last else F32
        return call(
            lambda *refs: query_side_kernel(len(held), not sums, *refs),
            [shape(rows, DL, dtype), shape(rows, QKW if last else WIDE, dtype)],
            [VMEM] * len(args),
            args,
        )

    def add(here, come, half=None, beside=None):
        args = [here, come] + ([] if beside is None else [beside])
        return call(
            lambda *refs: add_kernel(half, *refs),
            shape(*here.shape, BF16),
            [VMEM] * len(args),
            args,
        )

    r1, l1 = right(pair), left(pair)
    r1, q, do = after(r1, q, do)
    r2, l2 = right(r1), left(l1)
    stats = take_stats([pair], None)
    stats = take_stats([r1, l1], stats)
    r2, stats = after(r2, stats)
    r3, l3 = right(r2), left(l2)
    stats = take_stats([r2, l2], stats)
    r3, stats = after(r3, stats)
    r4, l4 = right(r3[:own]), left(l3[own:])
    stats = take_stats([r3, l3], stats)
    stats = take_stats([r4, l4], stats)

    kr4, kl4, g4 = key_grads([r4, l4])
    ahead, behind = right(kr4), left(kl4)
    kr3, kl3, g3 = key_grads([r3, l3])
    ahead, behind = right(add(kl3, ahead, half=0)), left(add(kr3, behind, half=1))
    kr2, kl2, g2 = key_grads([r2, l2])
    kr1, kl1, g1 = key_grads([r1, l1])
    here, g0 = key_grads([pair])
    mine, beside = call(
        gain_kernel,
        [shape(1, DL, F32), shape(16, WIDE - QKW, BF16)],
        [SMEM] + [VMEM] * 6,
        (section, gain, g4, g3, g2, g1, g0),
    )
    ahead = right(add(kl2, ahead, beside=beside))
    behind = left(add(kr2, behind, beside=beside))
    sums = query_side([pair, r1], ())
    near = call(near_kernel, shape(1, DL, F32), [VMEM] * 3, (mine, ahead, behind))
    ahead, *sums = after(ahead, *sums)
    ahead, behind = right(add(kl1, ahead)), left(add(kr1, behind))
    across = swap(near, "z", n_z // 2)
    sums = query_side([l1, r2, l2], sums)
    here, *sums = after(here, *sums)
    mine, other, gain_sum = call(
        total_kernel,
        [shape(own, WIDE, F32), shape(own, WIDE, BF16), shape(1, DL, F32)],
        [SMEM] + [VMEM] * 5,
        (place, ahead, behind, here, near, across),
    )
    other = swap(other, "x", 1)
    att, dq = query_side([r3, l3, r4, l4], sums, last=True)
    other, att, dq = after(other, att, dq)
    latent_grad, rope_grad, gain_sum = call(
        latent_kernel,
        [shape(own, DL, BF16), shape(own, DR, BF16), shape(1, DL, F32)],
        [SMEM] + [VMEM] * 5,
        (section, mine, other, latent[0], gain, gain_sum),
    )
    gain_sum = gain_sum + swap(gain_sum, "pipe", n_pipe - 1)
    return (
        att.reshape(1, tokens, HEADS * DL),
        dq.reshape(1, tokens, HEADS * QKW),
        latent_grad[None],
        rope_grad[None],
        gain_sum,
    )


def solution(mesh):
    n_pipe, n_ctx = mesh.devices.shape
    split = Mesh(mesh.devices.reshape(n_pipe, n_ctx // 2, 2), ("pipe", "z", "x"))
    tokens = P("pipe", ("z", "x"), None)
    ints = P("pipe", ("z", "x"))
    return jax.shard_map(
        shards,
        mesh=split,
        in_specs=(tokens, tokens, tokens, tokens, P(), ints, ints),
        out_specs=(tokens, tokens, tokens, tokens, P("pipe", None)),
        check_vma=False,
    )
```

```python
import math

import jax
import jax.numpy as jnp
from jax import lax
from jax.experimental import pallas as pl
from jax.experimental.pallas import tpu as pltpu
from jax.sharding import Mesh, PartitionSpec as P

HEADS = 64
DL = 512
DR = 64
QKW = DL + DR
WIDE = 640
BLOCK = 64
SCORE_SCALE = 1.0 / math.sqrt(192.0)
F32 = jnp.float32
BF16 = jnp.bfloat16
VMEM = pl.BlockSpec(memory_space=pltpu.VMEM)
HBM = pl.BlockSpec(memory_space=pltpu.HBM)
SMEM = pl.BlockSpec(memory_space=pltpu.SMEM)


def call(kernel, out, ins, args, scratch=(), limit=16):
    return pl.pallas_call(
        kernel,
        out_shape=out,
        in_specs=ins,
        out_specs=jax.tree.map(lambda _: VMEM, out),
        scratch_shapes=scratch,
        compiler_params=pltpu.CompilerParams(vmem_limit_bytes=limit * 1024 * 1024),
        cost_estimate=pl.CostEstimate(flops=1, bytes_accessed=1, transcendentals=0),
    )(*args)


def shape(rows, columns, dtype):
    return jax.ShapeDtypeStruct((rows, columns), dtype)


def nt_dot(a, b):
    return lax.dot_general(a, b, (((1,), (1,)), ((), ())), preferred_element_type=F32)


def tn_dot(a, b):
    return lax.dot_general(a, b, (((0,), (0,)), ((), ())), preferred_element_type=F32)


def mm(a, b):
    return jnp.dot(a, b, preferred_element_type=F32)


def section_gain(gain_ref, section_ref):
    return gain_ref[pl.ds(section_ref[0], 1), :]


def fold(value, combine):
    parts = [value[i * 8 : (i + 1) * 8] for i in range(value.shape[0] // 8)]
    while len(parts) > 1:
        half = len(parts) // 2
        parts = [combine(parts[i], parts[half + i]) for i in range(half)]
    return parts[0]


def key_kernel(section_ref, blocks_in, latent_in, rope_in, gain_in, keys_ref, *scratch):
    blocks_ref, latent_ref, rope_ref, gain_ref, sems = scratch
    copies = [
        pltpu.make_async_copy(source, target, sems.at[i])
        for i, (source, target) in enumerate(
            zip((latent_in, rope_in, gain_in, blocks_in), (latent_ref, rope_ref, gain_ref, blocks_ref))
        )
    ]
    for copy in copies:
        copy.start()
    for copy in copies:
        copy.wait()
    own = keys_ref.shape[0]
    latent = latent_ref[...].astype(F32)
    inverse = lax.rsqrt(jnp.mean(latent * latent, axis=-1, keepdims=True) + 1e-06)
    keys_ref[:, :DL] = (latent * inverse * section_gain(gain_ref, section_ref)).astype(BF16)
    keys_ref[:, DL:QKW] = rope_ref[...].astype(F32).T.astype(BF16)
    first = lax.broadcasted_iota(jnp.int32, (own, WIDE - QKW), 0) < BLOCK
    blocks = jnp.where(first, blocks_ref[0, 0], blocks_ref[0, 1])
    keys_ref[:, QKW:] = blocks.astype(F32).astype(BF16)


def masked_scores(q_pos, q, k_ref):
    count = k_ref.shape[0]
    scores = nt_dot(k_ref[...], q) * SCORE_SCALE
    place = (lax.broadcasted_iota(jnp.int32, (count, 1), 0) % BLOCK).astype(F32)
    k_pos = k_ref[:, QKW : QKW + 1].astype(F32) * BLOCK + place
    return jnp.where(k_pos <= q_pos, scores, -jnp.inf)


def stats_kernel(first, parts, *refs):
    pos_ref, q_ref, do_ref = refs[:3]
    k_refs = refs[3 : 3 + parts]
    out_ref = refs[-1]
    q_pos = pos_ref[0:1, :]
    scores = [masked_scores(q_pos, q_ref[...], k_ref) for k_ref in k_refs]
    top = fold(jnp.concatenate([fold(s, jnp.maximum) for s in scores]), jnp.maximum)
    top = jnp.max(top, axis=0, keepdims=True)
    if not first:
        old = refs[3 + parts]
        top = jnp.maximum(top, old[0:1, :])
    total, pull = 0.0, 0.0
    for s, k_ref in zip(scores, k_refs):
        dprob = nt_dot(k_ref[:, :DL], do_ref[...])
        expo = jnp.exp(s - top)
        total = total + fold(expo, jnp.add)
        pull = pull + fold(expo * dprob, jnp.add)
    total = jnp.sum(total, axis=0, keepdims=True)
    pull = jnp.sum(pull, axis=0, keepdims=True)
    if not first:
        shrink = jnp.exp(old[0:1, :] - top)
        total = total + old[1:2, :] * shrink
        pull = pull + old[2:3, :] * shrink
    out_ref[0:1, :] = top
    out_ref[1:2, :] = total
    out_ref[2:3, :] = pull


def weights_of(stats_ref, pos_ref, q_ref, k_ref):
    scores = masked_scores(pos_ref[0:1, :], q_ref[...], k_ref)
    return jnp.exp(scores - stats_ref[0:1, :]) * (1.0 / stats_ref[1:2, :])


def dscore_of(weights, stats_ref, do_ref, k_ref):
    delta = stats_ref[2:3, :] * (1.0 / stats_ref[1:2, :])
    dprob = nt_dot(k_ref[:, :DL], do_ref[...])
    return (weights * (dprob - delta) * SCORE_SCALE).astype(BF16)


def key_grad_kernel(parts, *refs):
    pos_ref, stats_ref, q_ref, do_ref = refs[:4]
    k_refs = refs[4 : 4 + parts]
    kg_refs = refs[4 + parts : -1]
    split = len(kg_refs) // parts
    gain_sum = 0.0
    for i, k_ref in enumerate(k_refs):
        weights = weights_of(stats_ref, pos_ref, q_ref, k_ref)
        dscore = dscore_of(weights, stats_ref, do_ref, k_ref)
        weights = weights.astype(BF16)
        lat = mm(dscore, q_ref[:, :DL]) + mm(weights, do_ref[...])
        rope = mm(dscore, q_ref[:, DL:])
        for j, kg_ref in enumerate(kg_refs[i * split : (i + 1) * split]):
            at = slice(j * kg_ref.shape[0], (j + 1) * kg_ref.shape[0])
            kg_ref[:, :DL] = lat[at].astype(BF16)
            kg_ref[:, DL:] = rope[at].astype(BF16)
        gain_sum = gain_sum + fold(lat * k_ref[:, :DL].astype(F32), jnp.add)
    refs[-1][...] = gain_sum


def query_side_kernel(*refs):
    pos_ref, stats_ref, q_ref, do_ref = refs[:4]
    att_ref, dq_ref = refs[-2:]
    att, dq = 0.0, 0.0
    for k_ref in refs[4:-2]:
        weights = weights_of(stats_ref, pos_ref, q_ref, k_ref)
        dscore = dscore_of(weights, stats_ref, do_ref, k_ref)
        att = att + tn_dot(weights.astype(BF16), k_ref[:, :DL])
        dq = dq + tn_dot(dscore, k_ref[...])
    att_ref[...] = att
    dq_ref[...] = dq[:, :QKW]


def spread(vector):
    high = vector.astype(BF16).astype(F32)
    rows = [part[:, i : i + 64] for part in (high, vector - high) for i in range(0, DL, 64)]
    return jnp.concatenate(rows, axis=0).astype(BF16)


def gathered(ref):
    both = ref[0:16, QKW:].astype(F32)
    both = both[0:8] + both[8:16]
    return jnp.concatenate([both[i : i + 1] for i in range(8)], axis=1)


def gain_kernel(section_ref, gain_ref, *refs):
    total = refs[0][...]
    for ref in refs[1:-2]:
        total = total + ref[...]
    vector = jnp.sum(total, axis=0, keepdims=True) / section_gain(gain_ref, section_ref)
    refs[-2][...] = vector
    refs[-1][...] = spread(vector)


def add_kernel(half, here_ref, come_ref, *refs):
    out_ref = refs[-1]
    if half is None:
        out_ref[...] = (here_ref[...].astype(F32) + come_ref[...].astype(F32)).astype(BF16)
    else:
        own = come_ref.shape[0]
        at, rest = pl.ds(half * own, own), pl.ds((1 - half) * own, own)
        out_ref[at, :] = (here_ref[at, :].astype(F32) + come_ref[...].astype(F32)).astype(BF16)
        out_ref[rest, :] = here_ref[rest, :]
    if len(refs) > 1:
        out_ref[0:16, QKW:] = refs[0][...]


def near_kernel(own_ref, right_ref, left_ref, out_ref):
    out_ref[...] = own_ref[...] + gathered(right_ref) + gathered(left_ref)


def total_kernel(
    x_ref, right_ref, left_ref, here_ref, near_ref, across_ref, own_ref, far_ref, sum_ref
):
    own = own_ref.shape[0]
    for ref, place in ((own_ref, x_ref[0]), (far_ref, 1 - x_ref[0])):
        at = pl.ds(pl.multiple_of(place * own, own), own)
        ref[...] = (
            right_ref[at, :].astype(F32) + left_ref[at, :].astype(F32) + here_ref[at, :].astype(F32)
        ).astype(ref.dtype)
    total = near_ref[...] + across_ref[...] + gathered(right_ref) + gathered(left_ref)
    sum_ref[...] = total
    far_ref[0:16, QKW:] = spread(total)


def latent_kernel(section_ref, own_ref, far_ref, latent_ref, gain_ref, sum_ref, lg_ref, rg_ref, gg_ref):
    gain = section_gain(gain_ref, section_ref)
    latent = latent_ref[...].astype(F32)
    inverse = lax.rsqrt(jnp.mean(latent * latent, axis=-1, keepdims=True) + 1e-06)
    total = own_ref[...] + far_ref[...].astype(F32)
    gated = total[:, :DL] * gain
    mean = jnp.mean(gated * latent, axis=-1, keepdims=True)
    lg_ref[...] = (inverse * gated - latent * (inverse * inverse * inverse) * mean).astype(BF16)
    rg_ref[...] = total[:, DL:QKW].T.astype(BF16)
    gg_ref[...] = sum_ref[...] + gathered(far_ref)


def after(value, *first):
    return lax.optimization_barrier((value, *first))


def swap(value, axis, mask):
    size = lax.axis_size(axis)
    return lax.ppermute(value, axis, [(i, i ^ mask) for i in range(size)])


def shards(queries, out_grad, latent, rope_keys, gain, block_map, query_start):
    tokens = queries.shape[1]
    rows = tokens * HEADS
    own = latent.shape[1]
    n_pipe = lax.axis_size("pipe")
    n_z = lax.axis_size("z")
    pipe = lax.axis_index("pipe")
    section = jnp.minimum(pipe, n_pipe - 1 - pipe).reshape(1)
    place = lax.axis_index("x").reshape(1)

    def right(value):
        return lax.ppermute(value, "z", [(i, (i + 1) % n_z) for i in range(n_z)])

    def left(value):
        return lax.ppermute(value, "z", [(i, (i - 1) % n_z) for i in range(n_z)])

    local = call(
        key_kernel,
        shape(own, WIDE, BF16),
        [SMEM, HBM, HBM, HBM, HBM],
        (section, block_map, latent[0], rope_keys[0].T, gain),
        [
            pltpu.SMEM(block_map.shape, jnp.int32),
            pltpu.VMEM((own, DL), BF16),
            pltpu.VMEM((DR, own), BF16),
            pltpu.VMEM(gain.shape, F32),
            pltpu.SemaphoreType.DMA((4,)),
        ],
        limit=60,
    )
    pair = lax.all_gather(local, "x", axis=0, tiled=True)
    q = jnp.pad(queries[0].reshape(rows, QKW), ((0, 0), (0, WIDE - QKW)))
    do = out_grad[0].reshape(rows, DL)
    token = jnp.arange(8 * rows, dtype=jnp.int32).reshape(8, rows) % rows // HEADS
    q_pos = (query_start[0, 0] + token).astype(F32)

    def take_stats(held, stats):
        args = [q_pos, q, do, *held] + ([] if stats is None else [stats])
        return call(
            lambda *refs: stats_kernel(stats is None, len(held), *refs),
            shape(8, rows, F32),
            [VMEM] * len(args),
            args,
        )

    def key_grads(held, split=1):
        args = [q_pos, stats, q, do, *held]
        sizes = [piece.shape[0] // split for piece in held for _ in range(split)]
        return call(
            lambda *refs: key_grad_kernel(len(held), *refs),
            [shape(size, WIDE, BF16) for size in sizes] + [shape(8, DL, F32)],
            [VMEM] * len(args),
            args,
        )

    def query_side(held):
        args = [q_pos, stats, q, do, *held]
        out = [shape(rows, DL, F32), shape(rows, QKW, F32)]
        return call(query_side_kernel, out, [VMEM] * len(args), args)

    def add(here, come, half=None, beside=None):
        args = [here, come] + ([] if beside is None else [beside])
        return call(
            lambda *refs: add_kernel(half, *refs),
            shape(*here.shape, BF16),
            [VMEM] * len(args),
            args,
        )

    r1, l1 = right(pair), left(pair)
    r1, q, do = after(r1, q, do)
    r2, l2 = right(r1), left(l1)
    stats = take_stats([pair], None)
    stats = take_stats([r1, l1], stats)
    r2, stats = after(r2, stats)
    r3, l3 = right(r2), left(l2)
    stats = take_stats([r2, l2], stats)
    r3, stats = after(r3, stats)
    r4, l4 = right(r3[:own]), left(l3[own:])
    stats = take_stats([r3, l3], stats)
    stats = take_stats([r4, l4], stats)

    kr4, kl4, g4 = key_grads([r4, l4])
    ahead, behind = right(kr4), left(kl4)
    kr3, kl3, g3 = key_grads([r3, l3])
    ahead, behind = right(add(kl3, ahead, half=0)), left(add(kr3, behind, half=1))
    kr2, kl2, g2 = key_grads([r2, l2])
    kr1, kl1, g1 = key_grads([r1, l1])
    here, g0 = key_grads([pair])
    mine, beside = call(
        gain_kernel,
        [shape(1, DL, F32), shape(16, WIDE - QKW, BF16)],
        [SMEM] + [VMEM] * 6,
        (section, gain, g4, g3, g2, g1, g0),
    )
    ahead = right(add(kl2, ahead, beside=beside))
    behind = left(add(kr2, behind, beside=beside))
    first = query_side([pair, r1, l1, r2])
    near = call(near_kernel, shape(1, DL, F32), [VMEM] * 3, (mine, ahead, behind))
    ahead, *first = after(ahead, *first)
    ahead, behind = right(add(kl1, ahead)), left(add(kr1, behind))
    across = swap(near, "z", n_z // 2)
    mine, other, gain_sum = call(
        total_kernel,
        [shape(own, WIDE, F32), shape(own, WIDE, BF16), shape(1, DL, F32)],
        [SMEM] + [VMEM] * 5,
        (place, ahead, behind, here, near, across),
    )
    other = swap(other, "x", 1)
    second = query_side([l2, r3, l3, r4, l4])
    other, *second = after(other, *second)
    latent_grad, rope_grad, gain_sum = call(
        latent_kernel,
        [shape(own, DL, BF16), shape(DR, own, BF16), shape(1, DL, F32)],
        [SMEM] + [VMEM] * 5,
        (section, mine, other, latent[0], gain, gain_sum),
    )
    gain_sum = gain_sum + swap(gain_sum, "pipe", n_pipe - 1)
    return (
        *((a + b).astype(BF16).reshape(1, tokens, -1) for a, b in zip(first, second)),
        latent_grad[None],
        rope_grad.T[None],
        gain_sum,
    )


def solution(mesh):
    n_pipe, n_ctx = mesh.devices.shape
    split = Mesh(mesh.devices.reshape(n_pipe, n_ctx // 2, 2), ("pipe", "z", "x"))
    tokens = P("pipe", ("z", "x"), None)
    ints = P("pipe", ("z", "x"))
    return jax.shard_map(
        shards,
        mesh=split,
        in_specs=(tokens, tokens, tokens, tokens, P(), ints, ints),
        out_specs=(tokens, tokens, tokens, tokens, P("pipe", None)),
        check_vma=False,
    )
```

```python
import math

import jax
import jax.numpy as jnp
from jax import lax
from jax.experimental import pallas as pl
from jax.experimental.pallas import tpu as pltpu
from jax.sharding import Mesh, PartitionSpec as P

HEADS = 64
DL = 512
DR = 64
QKW = DL + DR
WIDE = 640
BLOCK = 64
SCORE_SCALE = 1.0 / math.sqrt(192.0)
F32 = jnp.float32
BF16 = jnp.bfloat16
VMEM = pl.BlockSpec(memory_space=pltpu.VMEM)
HBM = pl.BlockSpec(memory_space=pltpu.HBM)
SMEM = pl.BlockSpec(memory_space=pltpu.SMEM)


def call(kernel, out, ins, args, scratch=(), limit=16):
    return pl.pallas_call(
        kernel,
        out_shape=out,
        in_specs=ins,
        out_specs=jax.tree.map(lambda _: VMEM, out),
        scratch_shapes=scratch,
        compiler_params=pltpu.CompilerParams(vmem_limit_bytes=limit * 1024 * 1024),
        cost_estimate=pl.CostEstimate(flops=1, bytes_accessed=1, transcendentals=0),
    )(*args)


def shape(rows, columns, dtype):
    return jax.ShapeDtypeStruct((rows, columns), dtype)


def nt_dot(a, b):
    return lax.dot_general(a, b, (((1,), (1,)), ((), ())), preferred_element_type=F32)


def tn_dot(a, b):
    return lax.dot_general(a, b, (((0,), (0,)), ((), ())), preferred_element_type=F32)


def mm(a, b):
    return jnp.dot(a, b, preferred_element_type=F32)


def section_gain(gain_ref, section_ref):
    return gain_ref[pl.ds(section_ref[0], 1), :]


def fold(value, combine):
    parts = [value[i * 8 : (i + 1) * 8] for i in range(value.shape[0] // 8)]
    while len(parts) > 1:
        half = len(parts) // 2
        parts = [combine(parts[i], parts[half + i]) for i in range(half)]
    return parts[0]


def key_kernel(section_ref, blocks_in, latent_in, rope_in, gain_in, keys_ref, *scratch):
    blocks_ref, latent_ref, rope_ref, gain_ref, sems = scratch
    copies = [
        pltpu.make_async_copy(source, target, sems.at[i])
        for i, (source, target) in enumerate(
            zip((latent_in, rope_in, gain_in, blocks_in), (latent_ref, rope_ref, gain_ref, blocks_ref))
        )
    ]
    for copy in copies:
        copy.start()
    for copy in copies:
        copy.wait()
    own = keys_ref.shape[0]
    latent = latent_ref[...].astype(F32)
    inverse = lax.rsqrt(jnp.mean(latent * latent, axis=-1, keepdims=True) + 1e-06)
    keys_ref[:, :DL] = (latent * inverse * section_gain(gain_ref, section_ref)).astype(BF16)
    keys_ref[:, DL:QKW] = rope_ref[...].astype(F32).T.astype(BF16)
    first = lax.broadcasted_iota(jnp.int32, (own, WIDE - QKW), 0) < BLOCK
    blocks = jnp.where(first, blocks_ref[0, 0], blocks_ref[0, 1])
    keys_ref[:, QKW:] = blocks.astype(F32).astype(BF16)


def masked_scores(q_pos, q, k_ref):
    count = k_ref.shape[0]
    scores = nt_dot(k_ref[...], q) * SCORE_SCALE
    place = (lax.broadcasted_iota(jnp.int32, (count, 1), 0) % BLOCK).astype(F32)
    k_pos = k_ref[:, QKW : QKW + 1].astype(F32) * BLOCK + place
    return jnp.where(k_pos <= q_pos, scores, -jnp.inf)


def take_stats(q_pos, q_ref, do_ref, k_refs, old):
    scores = [masked_scores(q_pos, q_ref[...], k_ref) for k_ref in k_refs]
    top = fold(jnp.concatenate([fold(s, jnp.maximum) for s in scores]), jnp.maximum)
    top = jnp.max(top, axis=0, keepdims=True)
    if old is not None:
        top = jnp.maximum(top, old[0:1, :])
    total, pull, kept = 0.0, 0.0, []
    for s, k_ref in zip(scores, k_refs):
        dprob = nt_dot(k_ref[:, :DL], do_ref[...])
        expo = jnp.exp(s - top)
        kept.append((expo, dprob))
        total = total + fold(expo, jnp.add)
        pull = pull + fold(expo * dprob, jnp.add)
    total = jnp.sum(total, axis=0, keepdims=True)
    pull = jnp.sum(pull, axis=0, keepdims=True)
    if old is not None:
        shrink = jnp.exp(old[0:1, :] - top)
        total = total + old[1:2, :] * shrink
        pull = pull + old[2:3, :] * shrink
    return top, total, pull, kept


def stats_kernel(first, parts, *refs):
    pos_ref, q_ref, do_ref = refs[:3]
    old = None if first else refs[3 + parts]
    out_ref = refs[-1]
    rows = take_stats(pos_ref[0:1, :], q_ref, do_ref, refs[3 : 3 + parts], old)
    for i in range(3):
        out_ref[i : i + 1, :] = rows[i]


def last_kernel(pos_ref, q_ref, do_ref, near_ref, far_ref, old_ref, out_ref, *outs):
    k_refs = (near_ref, far_ref)
    top, total, pull, kept = take_stats(pos_ref[0:1, :], q_ref, do_ref, k_refs, old_ref)
    for i, row in enumerate((top, total, pull)):
        out_ref[i : i + 1, :] = row
    scale = 1.0 / total
    delta = pull * scale
    gain_sum = 0.0
    for (expo, dprob), k_ref, kg_ref in zip(kept, k_refs, outs):
        weights = expo * scale
        dscore = (weights * (dprob - delta) * SCORE_SCALE).astype(BF16)
        gain_sum = gain_sum + key_grad(weights.astype(BF16), dscore, q_ref, do_ref, k_ref, kg_ref)
    outs[-1][...] = gain_sum


def key_grad(weights, dscore, q_ref, do_ref, k_ref, kg_ref):
    lat = mm(dscore, q_ref[:, :DL]) + mm(weights, do_ref[...])
    kg_ref[:, :DL] = lat.astype(BF16)
    kg_ref[:, DL:] = mm(dscore, q_ref[:, DL:]).astype(BF16)
    return fold(lat * k_ref[:, :DL].astype(F32), jnp.add)


def weights_of(stats_ref, pos_ref, q_ref, k_ref):
    scores = masked_scores(pos_ref[0:1, :], q_ref[...], k_ref)
    return jnp.exp(scores - stats_ref[0:1, :]) * (1.0 / stats_ref[1:2, :])


def dscore_of(weights, stats_ref, do_ref, k_ref):
    delta = stats_ref[2:3, :] * (1.0 / stats_ref[1:2, :])
    dprob = nt_dot(k_ref[:, :DL], do_ref[...])
    return (weights * (dprob - delta) * SCORE_SCALE).astype(BF16)


def key_grad_kernel(parts, *refs):
    pos_ref, stats_ref, q_ref, do_ref = refs[:4]
    k_refs = refs[4 : 4 + parts]
    gain_sum = 0.0
    for k_ref, kg_ref in zip(k_refs, refs[4 + parts :]):
        weights = weights_of(stats_ref, pos_ref, q_ref, k_ref)
        dscore = dscore_of(weights, stats_ref, do_ref, k_ref)
        gain_sum = gain_sum + key_grad(weights.astype(BF16), dscore, q_ref, do_ref, k_ref, kg_ref)
    refs[-1][...] = gain_sum


def query_side_kernel(*refs):
    pos_ref, stats_ref, q_ref, do_ref = refs[:4]
    att_ref, dq_ref = refs[-2:]
    att, dq = 0.0, 0.0
    for k_ref in refs[4:-2]:
        weights = weights_of(stats_ref, pos_ref, q_ref, k_ref)
        dscore = dscore_of(weights, stats_ref, do_ref, k_ref)
        att = att + tn_dot(weights.astype(BF16), k_ref[:, :DL])
        dq = dq + tn_dot(dscore, k_ref[...])
    att_ref[...] = att
    dq_ref[...] = dq[:, :QKW]


def spread(vector):
    high = vector.astype(BF16).astype(F32)
    rows = [part[:, i : i + 64] for part in (high, vector - high) for i in range(0, DL, 64)]
    return jnp.concatenate(rows, axis=0).astype(BF16)


def gathered(ref):
    both = ref[0:16, QKW:].astype(F32)
    both = both[0:8] + both[8:16]
    return jnp.concatenate([both[i : i + 1] for i in range(8)], axis=1)


def gain_kernel(section_ref, gain_ref, *refs):
    total = refs[0][...]
    for ref in refs[1:-2]:
        total = total + ref[...]
    vector = jnp.sum(total, axis=0, keepdims=True) / section_gain(gain_ref, section_ref)
    refs[-2][...] = vector
    refs[-1][...] = spread(vector)


def add_kernel(half, here_ref, come_ref, *refs):
    out_ref = refs[-1]
    if half is None:
        out_ref[...] = (here_ref[...].astype(F32) + come_ref[...].astype(F32)).astype(BF16)
    else:
        own = come_ref.shape[0]
        at, rest = pl.ds(half * own, own), pl.ds((1 - half) * own, own)
        out_ref[at, :] = (here_ref[at, :].astype(F32) + come_ref[...].astype(F32)).astype(BF16)
        out_ref[rest, :] = here_ref[rest, :]
    if len(refs) > 1:
        out_ref[0:16, QKW:] = refs[0][...]


def near_kernel(own_ref, right_ref, left_ref, out_ref):
    out_ref[...] = own_ref[...] + gathered(right_ref) + gathered(left_ref)


def total_kernel(
    x_ref, right_ref, left_ref, here_ref, near_ref, across_ref, own_ref, far_ref, sum_ref
):
    own = own_ref.shape[0]
    for ref, place in ((own_ref, x_ref[0]), (far_ref, 1 - x_ref[0])):
        at = pl.ds(pl.multiple_of(place * own, own), own)
        ref[...] = (
            right_ref[at, :].astype(F32) + left_ref[at, :].astype(F32) + here_ref[at, :].astype(F32)
        ).astype(ref.dtype)
    total = near_ref[...] + across_ref[...] + gathered(right_ref) + gathered(left_ref)
    sum_ref[...] = total
    far_ref[0:16, QKW:] = spread(total)


def sum_kernel(sum_ref, far_ref, out_ref):
    out_ref[...] = sum_ref[...] + gathered(far_ref)


def plus_kernel(one_ref, two_ref, out_ref):
    out_ref[...] = one_ref[...] + two_ref[...]


def latent_kernel(section_ref, own_ref, far_ref, latent_ref, gain_ref, lg_ref, rg_ref):
    gain = section_gain(gain_ref, section_ref)
    latent = latent_ref[...].astype(F32)
    inverse = lax.rsqrt(jnp.mean(latent * latent, axis=-1, keepdims=True) + 1e-06)
    total = own_ref[...] + far_ref[...].astype(F32)
    gated = total[:, :DL] * gain
    mean = jnp.mean(gated * latent, axis=-1, keepdims=True)
    lg_ref[...] = (inverse * gated - latent * (inverse * inverse * inverse) * mean).astype(BF16)
    rg_ref[...] = total[:, DL:QKW].T.astype(BF16)


def after(value, *first):
    return lax.optimization_barrier((value, *first))


def swap(value, axis, mask):
    size = lax.axis_size(axis)
    return lax.ppermute(value, axis, [(i, i ^ mask) for i in range(size)])


def shards(queries, out_grad, latent, rope_keys, gain, block_map, query_start):
    tokens = queries.shape[1]
    rows = tokens * HEADS
    own = latent.shape[1]
    n_pipe = lax.axis_size("pipe")
    n_z = lax.axis_size("z")
    pipe = lax.axis_index("pipe")
    section = jnp.minimum(pipe, n_pipe - 1 - pipe).reshape(1)
    place = lax.axis_index("x").reshape(1)

    def right(value):
        return lax.ppermute(value, "z", [(i, (i + 1) % n_z) for i in range(n_z)])

    def left(value):
        return lax.ppermute(value, "z", [(i, (i - 1) % n_z) for i in range(n_z)])

    local = call(
        key_kernel,
        shape(own, WIDE, BF16),
        [SMEM, HBM, HBM, HBM, HBM],
        (section, block_map, latent[0], rope_keys[0].T, gain),
        [
            pltpu.SMEM(block_map.shape, jnp.int32),
            pltpu.VMEM((own, DL), BF16),
            pltpu.VMEM((DR, own), BF16),
            pltpu.VMEM(gain.shape, F32),
            pltpu.SemaphoreType.DMA((4,)),
        ],
        limit=60,
    )
    pair = lax.all_gather(local, "x", axis=0, tiled=True)
    q = jnp.pad(queries[0].reshape(rows, QKW), ((0, 0), (0, WIDE - QKW)))
    do = out_grad[0].reshape(rows, DL)
    token = jnp.arange(8 * rows, dtype=jnp.int32).reshape(8, rows) % rows // HEADS
    q_pos = (query_start[0, 0] + token).astype(F32)

    def add_stats(held, stats):
        args = [q_pos, q, do, *held] + ([] if stats is None else [stats])
        return call(
            lambda *refs: stats_kernel(stats is None, len(held), *refs),
            shape(8, rows, F32),
            [VMEM] * len(args),
            args,
        )

    def key_grads(held):
        args = [q_pos, stats, q, do, *held]
        return call(
            lambda *refs: key_grad_kernel(len(held), *refs),
            [shape(piece.shape[0], WIDE, BF16) for piece in held] + [shape(8, DL, F32)],
            [VMEM] * len(args),
            args,
        )

    def query_side(held):
        args = [q_pos, stats, q, do, *held]
        out = [shape(rows, DL, F32), shape(rows, QKW, F32)]
        return call(query_side_kernel, out, [VMEM] * len(args), args)

    def add(here, come, half=None, beside=None):
        args = [here, come] + ([] if beside is None else [beside])
        return call(
            lambda *refs: add_kernel(half, *refs),
            shape(*here.shape, BF16),
            [VMEM] * len(args),
            args,
        )

    r1, l1 = right(pair), left(pair)
    r1, q, do = after(r1, q, do)
    r2, l2 = right(r1), left(l1)
    stats = add_stats([pair], None)
    stats = add_stats([r1, l1], stats)
    r2, stats = after(r2, stats)
    r3, l3 = right(r2), left(l2)
    stats = add_stats([r2, l2], stats)
    r3, stats = after(r3, stats)
    r4, l4 = right(r3[:own]), left(l3[own:])
    stats = add_stats([r3, l3], stats)

    args = (q_pos, q, do, r4, l4, stats)
    stats, kr4, kl4, g4 = call(
        last_kernel,
        [shape(8, rows, F32), shape(own, WIDE, BF16), shape(own, WIDE, BF16), shape(8, DL, F32)],
        [VMEM] * len(args),
        args,
    )
    ahead, behind = right(kr4), left(kl4)
    kr3, kl3, g3 = key_grads([r3, l3])
    ahead, behind = right(add(kl3, ahead, half=0)), left(add(kr3, behind, half=1))
    kr2, kl2, g2 = key_grads([r2, l2])
    kr1, kl1, g1 = key_grads([r1, l1])
    here, g0 = key_grads([pair])
    mine, beside = call(
        gain_kernel,
        [shape(1, DL, F32), shape(16, WIDE - QKW, BF16)],
        [SMEM] + [VMEM] * 6,
        (section, gain, g4, g3, g2, g1, g0),
    )
    ahead = right(add(kl2, ahead, beside=beside))
    behind = left(add(kr2, behind, beside=beside))
    first = query_side([pair, r1, l1, r2])
    near = call(near_kernel, shape(1, DL, F32), [VMEM] * 3, (mine, ahead, behind))
    ahead, *first = after(ahead, *first)
    ahead, behind = right(add(kl1, ahead)), left(add(kr1, behind))
    across = swap(near, "z", n_z // 2)
    mine, other, gain_sum = call(
        total_kernel,
        [shape(own, WIDE, F32), shape(own, WIDE, BF16), shape(1, DL, F32)],
        [SMEM] + [VMEM] * 5,
        (place, ahead, behind, here, near, across),
    )
    other = swap(other, "x", 1)
    second = query_side([l2, r3, l3, r4, l4])
    other, *second = after(other, *second)
    gain_sum = call(sum_kernel, shape(1, DL, F32), [VMEM] * 2, (gain_sum, other))
    mirror = swap(gain_sum, "pipe", n_pipe - 1)
    other, gain_sum = after(other, gain_sum)
    latent_grad, rope_grad = call(
        latent_kernel,
        [shape(own, DL, BF16), shape(DR, own, BF16)],
        [SMEM] + [VMEM] * 4,
        (section, mine, other, latent[0], gain),
    )
    gain_sum = call(plus_kernel, shape(1, DL, F32), [VMEM] * 2, (gain_sum, mirror))
    return (
        *((a + b).astype(BF16).reshape(1, tokens, -1) for a, b in zip(first, second)),
        latent_grad[None],
        rope_grad.T[None],
        gain_sum,
    )


def solution(mesh):
    n_pipe, n_ctx = mesh.devices.shape
    split = Mesh(mesh.devices.reshape(n_pipe, n_ctx // 2, 2), ("pipe", "z", "x"))
    tokens = P("pipe", ("z", "x"), None)
    ints = P("pipe", ("z", "x"))
    return jax.shard_map(
        shards,
        mesh=split,
        in_specs=(tokens, tokens, tokens, tokens, P(), ints, ints),
        out_specs=(tokens, tokens, tokens, tokens, P("pipe", None)),
        check_vma=False,
    )
```
